32 devices in a mesh: series: 8 (over y, x, core), tm: 4 (over z).
Axes of the slice: x: 2, y: 2, z: 4, core: 2. Of those that a mesh axis runs over, the one named last changes fastest.
Arguments:
- metric: bfloat16 [8192, 4096], P('series', 'tm'), may hold values from -6 to 6
- omega: bfloat16 [4096, 256], P('tm'), may hold values from -0.09375 to 0.09375
- psi: bfloat16 [513, 8192], P(None, 'series'), may hold values from -0.0625 to 0.0625
- phi: bfloat16 [512, 8192], P(None, 'series'), may hold values from -0.0625 to 0.0625
- theta: bfloat16 [512, 4096], P(None, 'tm'), may hold values from -0.09375 to 0.09375
- range_old: float32 [8192, 256], P('series', 'tm'), may hold values from -6 to 6
- corange_old: float32 [513, 4096], P(None, ('tm', 'series')), may hold values from -6 to 6
- core_old: float32 [512, 512], replicated, may hold values from -6 to 6
Outputs:
- range_new: float32 [8192, 256], P('series', 'tm')
- corange_new: float32 [513, 4096], P(None, ('tm', 'series'))
- core_new: float32 [512, 512], replicated
The draws below stay inside these ranges and needn't reach their ends.
All inputs are finite; a program needn't handle non-finite values.
Results may differ from the reference program's by a relative error of at most 0.0003.
Values sent between devices are 32-bit elements; how exact they have to be, the bound alone decides.
No kernel may reach another device: no remote copies, remote signals or barrier semaphores. Data moves between devices by JAX's collectives and lax.ppermute only.
A program may use at most 64 MiB of HBM per device.

```python
import jax
import jax.numpy as jnp
from jax import lax

K = 256
L = 513
S = 512
M = 8192
N = 4096


def spiked(array, key, source, target, blocks, factor):
    owner, partner = [(jnp.arange(array.shape[axis_at]) // (array.shape[axis_at] // blocks)).reshape([-1 if axis == axis_at else 1 for axis in range(array.ndim)]) for axis_at in (source, target)]
    chosen = jax.random.permutation(key, blocks)[partner]
    strong = (owner == chosen) | (owner == (partner + blocks // 2) % blocks)
    return jnp.where(strong, factor * array, array)


def block_levels(stream_key, dims, split, smallest, largest):
    factor_of = 1.0
    for axis_at, blocks in split:
        heights = jax.random.uniform(jax.random.fold_in(jax.random.fold_in(stream_key, 6), axis_at), (blocks,), jnp.float32, smallest / len(split), largest / len(split))
        factor_of = factor_of * jnp.repeat(jnp.exp(heights), dims[axis_at] // blocks).reshape((-1,) + (1,) * (len(dims) - 1 - axis_at))
    return factor_of


def gaussian(own_key, dims, width, limit, split=(), held_as=jnp.bfloat16):
    result = jax.random.normal(own_key, dims, jnp.float32) * width
    if len(split) > 0:
        result = block_levels(own_key, dims, split, -0.22, 0.18) * result
    return jnp.clip(result, min=-limit, max=limit).astype(held_as)


def gaussian_with(stream_key, shape, width, most, shards, heavy, kind=jnp.bfloat16):
    entries = width * jax.random.normal(stream_key, shape, jnp.float32)
    if shards:
        entries = entries * block_levels(stream_key, shape, shards, -0.22, 0.18)
    return jnp.clip(spiked(entries, jax.random.fold_in(stream_key, 3), *heavy), -most, most).astype(kind)


def setup_inputs(seed: int = 0) -> dict:
    key_list = jax.random.split(jax.random.key(seed), 9)
    return {
        "metric": gaussian_with(key_list[0], (M, N), 1.0, 6.0, ((0, 8), (1, 4)), (0, 1, 8, 2.0)),
        "omega": gaussian(key_list[1], (N, K), N ** -0.5, 0.09375, ((0, 4),)),
        "psi": gaussian(key_list[2], (L, M), M ** -0.5, 0.0625, ((1, 8),)),
        "phi": gaussian(key_list[3], (S, M), M ** -0.5, 0.0625, ((1, 8),)),
        "theta": gaussian(key_list[4], (S, N), N ** -0.5, 0.09375, ((1, 4),)),
        "range_old": gaussian(key_list[5], (M, K), 1.0, 6.0, ((0, 8), (1, 4)), jnp.float32),
        "corange_old": gaussian(key_list[6], (L, N), 1.0, 6.0, ((1, 32),), jnp.float32),
        "core_old": gaussian(key_list[7], (S, S), 1.0, 6.0, (), jnp.float32),
    }


def reference(metric, omega, psi, phi, theta, range_old, corange_old, core_old):
    range_new = range_old + jnp.dot(metric, omega, preferred_element_type=jnp.float32)
    corange_new = corange_old + jnp.dot(psi, metric, preferred_element_type=jnp.float32)
    left = jnp.dot(phi, metric, preferred_element_type=jnp.float32)
    core_new = core_old + jnp.einsum("sc,tc->st", left, theta.astype(jnp.float32), precision=lax.Precision.HIGHEST)
    return range_new, corange_new, core_new
```

```python
import functools
import operator

import jax
import jax.numpy as jnp
from jax import lax
from jax.experimental import pallas as pl
from jax.experimental.pallas import tpu as pltpu
from jax.sharding import PartitionSpec as P

F32 = jnp.float32
RADIX = 4
VMEM_LIMIT = 48 * 1024 * 1024


def added(terms):
    return functools.reduce(operator.add, terms)


def swap(value, axis, bits, size):
    return lax.ppermute(value, axis, [(i, i ^ bits) for i in range(size)])


def params():
    return pltpu.CompilerParams(vmem_limit_bytes=VMEM_LIMIT)


def whole(shape):
    return pl.BlockSpec(shape, lambda i, at: (0,) * len(shape))


def core_kernel(parts, at_ref, phi_ref, metric_ref, theta_ref, out_ref, sum_ref):
    chip = at_ref[1]
    left = jnp.dot(phi_ref[...], metric_ref[...], preferred_element_type=F32)
    high = left.astype(jnp.bfloat16)
    low = (left - high.astype(F32)).astype(jnp.bfloat16)
    theta = theta_ref[...]
    by_rows = (((1,), (1,)), ((), ()))
    sum_ref[...] = lax.dot_general(high, theta, by_rows, preferred_element_type=F32)
    sum_ref[...] += lax.dot_general(low, theta, by_rows, preferred_element_type=F32)
    rows = sum_ref.shape[0] // parts
    for k in range(parts):
        first = pl.multiple_of((chip ^ k) * rows, rows)
        out_ref[k] = sum_ref[pl.ds(first, rows), :]


def core_half(half, chip, phi, metric, theta, parts):
    order, depth = phi.shape
    rows = order // 2
    cols = theta.shape[0]
    return pl.pallas_call(
        functools.partial(core_kernel, parts),
        grid_spec=pltpu.PrefetchScalarGridSpec(
            num_scalar_prefetch=1,
            grid=(1,),
            in_specs=[
                pl.BlockSpec((rows, depth), lambda i, at: (at[0], 0)),
                whole(metric.shape),
                whole(theta.shape),
            ],
            out_specs=whole((parts, rows // parts, cols)),
            scratch_shapes=[pltpu.VMEM((rows, cols), F32)],
        ),
        out_shape=jax.ShapeDtypeStruct((parts, rows // parts, cols), F32),
        compiler_params=params(),
        name="core_half",
    )(jnp.stack([half, chip]), phi, metric, theta)


def range_kernel(parts, at_ref, omega_ref, metric_ref, send_ref, far_ref, own_ref, sum_ref):
    slot = at_ref[0]
    sum_ref[...] = lax.dot_general(
        omega_ref[...], metric_ref[...], (((0,), (1,)), ((), ())), preferred_element_type=F32
    )
    rows = sum_ref.shape[0] // parts

    def block(k):
        return sum_ref[pl.ds(pl.multiple_of((slot ^ k) * rows, rows), rows), :]

    for j in range(parts // 2):
        send_ref[j] = block(2 * j + 1)
    for j in range(1, parts // 2):
        far_ref[j - 1] = block(2 * j)
    own_ref[...] = block(0)


def range_blocks(slot, omega, metric, parts):
    series, width = metric.shape[0], omega.shape[1]
    rows = width // parts
    shapes = [(parts // 2, rows, series), (parts // 2 - 1, rows, series), (rows, series)]
    return pl.pallas_call(
        functools.partial(range_kernel, parts),
        grid_spec=pltpu.PrefetchScalarGridSpec(
            num_scalar_prefetch=1,
            grid=(1,),
            in_specs=[whole(omega.shape), whole(metric.shape)],
            out_specs=[whole(s) for s in shapes],
            scratch_shapes=[pltpu.VMEM((width, series), F32)],
        ),
        out_shape=[jax.ShapeDtypeStruct(s, F32) for s in shapes],
        compiler_params=params(),
        name="range_blocks",
    )(jnp.stack([slot]), omega, metric)


def corange_kernel(at_ref, psi_ref, metric_ref, send_ref, keep_ref, sum_ref):
    core = at_ref[1]
    sum_ref[...] = jnp.dot(psi_ref[...], metric_ref[...], preferred_element_type=F32)
    cols = keep_ref.shape[2]
    keep_ref[0] = sum_ref[:, pl.ds(pl.multiple_of(core * cols, cols), cols)]
    send_ref[0] = sum_ref[:, pl.ds(pl.multiple_of((1 - core) * cols, cols), cols)]


def corange_blocks(core, chip, psi, metric, parts):
    rows, depth = psi.shape
    cols = metric.shape[1] // (2 * parts)
    if cols % 128:
        term = jnp.dot(psi, metric, preferred_element_type=F32).reshape(rows, parts, 2, cols)
        term = jnp.take(term, chip ^ jnp.arange(parts), axis=1)
        pick = lambda c: lax.dynamic_index_in_dim(term, c, 2, keepdims=False).transpose(1, 0, 2)
        return pick(1 - core), pick(core)
    shape = jax.ShapeDtypeStruct((parts, rows, cols), F32)
    block = pl.BlockSpec((1, rows, cols), lambda k, at: (k, 0, 0))
    return pl.pallas_call(
        corange_kernel,
        grid_spec=pltpu.PrefetchScalarGridSpec(
            num_scalar_prefetch=1,
            grid=(parts,),
            in_specs=[
                whole(psi.shape),
                pl.BlockSpec((depth, 2 * cols), lambda k, at: (0, at[0] ^ k)),
            ],
            out_specs=[block, block],
            scratch_shapes=[pltpu.VMEM((rows, 2 * cols), F32)],
        ),
        out_shape=[shape, shape],
        compiler_params=params(),
        name="corange_blocks",
    )(jnp.stack([chip, core]), psi, metric)


def place_kernel(rows, half, radix, at_ref, old_ref, *refs):
    core, chip = at_ref[0], at_ref[1]
    pieces, out_ref = refs[:-1], refs[-1]
    for i, ref in enumerate(pieces):
        side, digit = i // radix, i % radix
        for g in range(ref.shape[0]):
            row = ((core ^ side) * half + (chip ^ (g * radix + digit))) * rows
            at = pl.ds(pl.multiple_of(row, rows), rows)
            out_ref[at, :] = old_ref[at, :] + ref[g]


def placed(core, chip, old, pieces, parts):
    rows = old.shape[0] // (2 * parts)
    return pl.pallas_call(
        functools.partial(place_kernel, rows, parts, len(pieces) // 2),
        grid_spec=pltpu.PrefetchScalarGridSpec(
            num_scalar_prefetch=1,
            grid=(1,),
            in_specs=[whole(old.shape)] + [whole(p.shape) for p in pieces],
            out_specs=whole(old.shape),
        ),
        out_shape=jax.ShapeDtypeStruct(old.shape, F32),
        compiler_params=params(),
        name="placed",
    )(jnp.stack([core, chip]), old, *pieces)


def stages(chips):
    steps, stride = [], 1
    while stride < chips:
        radix = min(RADIX, chips // stride)
        steps.append((stride, radix))
        stride *= radix
    return steps


def sum_over_chips(terms, series):
    for stride, radix in stages(series // 2):
        left = terms[0].shape[0] // radix

        def digit(k):
            return added([t.reshape((left, radix) + t.shape[1:])[:, k] for t in terms])

        got = [swap(digit(k), "series", 2 * stride * k, series) for k in range(1, radix)]
        terms = [digit(0)] + got
    return terms


def gather_over_chips(own, series):
    held = [own]
    for stride, radix in reversed(stages(series // 2)):
        if len(held) > 1:
            own = jnp.stack(held, axis=1)
            own = own.reshape((-1,) + own.shape[2:])
        held = [own] + [swap(own, "series", 2 * stride * k, series) for k in range(1, radix)]
    return held


def body(series, tm, metric, omega, psi, phi, theta, range_old, corange_old, core_old):
    me = lax.axis_index("series")
    slot = lax.axis_index("tm")
    core, chip = me % 2, me // 2
    chips = series // 2

    core_send = core_half(1 - core, chip, phi, metric, theta, chips)
    core_got = swap(core_send, "series", 1, series)
    send, far, own = range_blocks(slot, omega, metric, tm)
    range_got = swap(send, "tm", 1, tm)
    core_keep = core_half(core, chip, phi, metric, theta, chips)
    core_terms = sum_over_chips([core_keep, core_got], series)

    corange_send, corange_keep = corange_blocks(core, chip, psi, metric, chips)
    corange_got = swap(corange_send, "series", 1, series)

    core_part = added(core_terms)
    parts = [core_part] + [swap(core_part, "tm", k, tm) for k in range(1, tm)]
    while len(parts) > 1:
        parts = [a + b for a, b in zip(parts[::2], parts[1::2])]

    own = own + range_got[0]
    far = far + range_got[1:]
    distance = 2
    while distance < tm:
        near, rest = far[::2], far[1::2]
        got = swap(near, "tm", distance, tm)
        own = own + got[0]
        far = rest + got[1:]
        distance *= 2
    range_new = range_old + own.T

    corange_terms = sum_over_chips([corange_keep, corange_got], series)

    pieces = gather_over_chips(parts[0], series)
    pieces = pieces + [swap(p, "series", 1, series) for p in pieces]
    core_new = placed(core, chip, core_old, pieces, chips)
    corange_new = corange_old + added(corange_terms)[0]
    return range_new, corange_new, core_new


def solution(mesh):
    return jax.shard_map(
        functools.partial(body, mesh.shape["series"], mesh.shape["tm"]),
        mesh=mesh,
        in_specs=(
            P("series", "tm"),
            P("tm", None),
            P(None, "series"),
            P(None, "series"),
            P(None, "tm"),
            P("series", "tm"),
            P(None, ("tm", "series")),
            P(),
        ),
        out_specs=(P("series", "tm"), P(None, ("tm", "series")), P()),
        check_vma=False,
    )
```

```python
import functools
import operator

import jax
import jax.numpy as jnp
from jax import lax
from jax.experimental import pallas as pl
from jax.experimental.pallas import tpu as pltpu
from jax.sharding import PartitionSpec as P

F32 = jnp.float32
RADIX = 4
CHUNKS = 4
DIRECT = True
VMEM_LIMIT = 8 * 1024 * 1024
BESIDE = pl.CostEstimate(flops=10**11, bytes_accessed=4 * 1024 * 1024, transcendentals=0)
FIRST_LIMIT = 60 * 1024 * 1024


def added(terms):
    return functools.reduce(operator.add, terms)


def swap(value, axis, bits, size):
    return lax.ppermute(value, axis, [(i, i ^ bits) for i in range(size)])


def params():
    return pltpu.CompilerParams(vmem_limit_bytes=VMEM_LIMIT)


def whole(shape):
    return pl.BlockSpec(shape, lambda i, at: (0,) * len(shape))


def core_kernel(
    parts, other, phi_any, metric_any, theta_any,
    out_ref, phi, metric, theta, high, low, sum_ref, sems,
):
    me = lax.axis_index("series")
    core, chip = me & 1, me >> 1
    rows, cols = phi.shape[0], metric.shape[1] // CHUNKS
    first = pl.multiple_of((core ^ other) * rows, rows)
    copies = [pltpu.make_async_copy(phi_any.at[pl.ds(first, rows), :], phi, sems.at[0])]
    for c in range(CHUNKS):
        at = slice(c * cols, (c + 1) * cols)
        copies.append(
            pltpu.make_async_copy(metric_any.at[:, at], metric.at[:, at], sems.at[1 + c])
        )
    copies.append(pltpu.make_async_copy(theta_any, theta, sems.at[1 + CHUNKS]))
    for copy in copies:
        copy.start()
    copies[0].wait()
    for c in range(CHUNKS):
        at = slice(c * cols, (c + 1) * cols)
        copies[1 + c].wait()
        left = jnp.dot(phi[...], metric[:, at], preferred_element_type=F32)
        top = left.astype(jnp.bfloat16)
        high[:, at] = top
        low[:, at] = (left - top.astype(F32)).astype(jnp.bfloat16)
    copies[-1].wait()
    by_rows = (((1,), (1,)), ((), ()))
    sum_ref[...] = lax.dot_general(high[...], theta[...], by_rows, preferred_element_type=F32)
    sum_ref[...] += lax.dot_general(low[...], theta[...], by_rows, preferred_element_type=F32)
    block = rows // parts
    for k in range(parts):
        out_ref[k] = sum_ref[pl.ds(pl.multiple_of((chip ^ k) * block, block), block), :]


def core_half(other, phi, metric, theta, parts):
    order, depth = phi.shape
    rows, cols = order // 2, theta.shape[0]
    left = (rows, metric.shape[1])
    shape = (parts, rows // parts, cols)
    return pl.pallas_call(
        functools.partial(core_kernel, parts, other),
        in_specs=[pl.BlockSpec(memory_space=pl.ANY)] * 3,
        out_specs=pl.BlockSpec(memory_space=pltpu.VMEM),
        scratch_shapes=[
            pltpu.VMEM((rows, depth), phi.dtype),
            pltpu.VMEM(metric.shape, metric.dtype),
            pltpu.VMEM(theta.shape, theta.dtype),
            pltpu.VMEM(left, jnp.bfloat16),
            pltpu.VMEM(left, jnp.bfloat16),
            pltpu.VMEM((rows, cols), F32),
            pltpu.SemaphoreType.DMA((CHUNKS + 2,)),
        ],
        out_shape=jax.ShapeDtypeStruct(shape, F32),
        compiler_params=pltpu.CompilerParams(vmem_limit_bytes=FIRST_LIMIT),
        name="core_half",
    )(phi, metric, theta)


def range_kernel(parts, at_ref, omega_ref, metric_ref, send_ref, far_ref, own_ref, sum_ref):
    slot = at_ref[0]
    sum_ref[...] = lax.dot_general(
        omega_ref[...], metric_ref[...], (((0,), (1,)), ((), ())), preferred_element_type=F32
    )
    rows = sum_ref.shape[0] // parts

    def block(k):
        return sum_ref[pl.ds(pl.multiple_of((slot ^ k) * rows, rows), rows), :]

    for j in range(parts // 2):
        send_ref[j] = block(2 * j + 1)
    for j in range(1, parts // 2):
        far_ref[j - 1] = block(2 * j)
    own_ref[...] = block(0)


def range_blocks(slot, omega, metric, parts):
    series, width = metric.shape[0], omega.shape[1]
    rows = width // parts
    shapes = [(parts // 2, rows, series), (parts // 2 - 1, rows, series), (rows, series)]
    return pl.pallas_call(
        functools.partial(range_kernel, parts),
        grid_spec=pltpu.PrefetchScalarGridSpec(
            num_scalar_prefetch=1,
            grid=(1,),
            in_specs=[whole(omega.shape), whole(metric.shape)],
            out_specs=[whole(s) for s in shapes],
            scratch_shapes=[pltpu.VMEM((width, series), F32)],
        ),
        out_shape=[jax.ShapeDtypeStruct(s, F32) for s in shapes],
        compiler_params=params(),
        name="range_blocks",
    )(jnp.stack([slot]), omega, metric)


def corange_kernel(parts, at_ref, psi_ref, metric_ref, *refs):
    chip, core = at_ref[0], at_ref[1]
    sent, kept, sum_ref = refs[:-1][: len(refs) // 2], refs[:-1][len(refs) // 2 :], refs[-1]
    rows, pair = sum_ref.shape
    cols = pair // 2
    for k in range(parts):
        first = pl.multiple_of((chip ^ k) * pair, pair)
        sum_ref[...] = jnp.dot(
            psi_ref[...], metric_ref[:, pl.ds(first, pair)], preferred_element_type=F32
        )
        for group, side in ((kept, core), (sent, 1 - core)):
            ref, j = group[k % len(group)], k // len(group)
            ref[j, :rows] = sum_ref[:, pl.ds(pl.multiple_of(side * cols, cols), cols)]
            if ref.shape[1] > rows:
                ref[j, rows:] = jnp.zeros((ref.shape[1] - rows, cols), F32)


def corange_blocks(core, chip, psi, metric, parts):
    rows, depth = psi.shape
    cols = metric.shape[1] // (2 * parts)
    radix = min(RADIX, parts)
    if cols % 128:
        term = jnp.dot(psi, metric, preferred_element_type=F32).reshape(rows, parts, 2, cols)
        term = jnp.take(term, chip ^ jnp.arange(parts), axis=1).transpose(2, 1, 0, 3)
        pick = lambda c: split(lax.dynamic_index_in_dim(term, c, 0, keepdims=False), radix)
        return pick(1 - core), pick(core)
    held = -(-rows // 8) * 8
    shape = (parts // radix, held, cols)
    blocks = pl.pallas_call(
        functools.partial(corange_kernel, parts),
        grid_spec=pltpu.PrefetchScalarGridSpec(
            num_scalar_prefetch=1,
            grid=(1,),
            in_specs=[whole(psi.shape), whole(metric.shape)],
            out_specs=[whole(shape)] * (2 * radix),
            scratch_shapes=[pltpu.VMEM((rows, 2 * cols), F32)],
        ),
        out_shape=[jax.ShapeDtypeStruct(shape, F32)] * (2 * radix),
        compiler_params=pltpu.CompilerParams(vmem_limit_bytes=2 * VMEM_LIMIT),
        cost_estimate=BESIDE,
        name="corange_blocks",
    )(jnp.stack([chip, core]), psi, metric)
    return blocks[:radix], blocks[radix:]


def range_add_kernel(own_ref, far_ref, got_ref, own_out, far_out):
    own_out[...] = own_ref[...] + got_ref[0]
    far_out[...] = far_ref[...] + got_ref[1:]


def range_add(own, far, got):
    vmem = pl.BlockSpec(memory_space=pltpu.VMEM)
    return pl.pallas_call(
        range_add_kernel,
        in_specs=[vmem] * 3,
        out_specs=[vmem] * 2,
        out_shape=[jax.ShapeDtypeStruct(a.shape, F32) for a in (own, far)],
        compiler_params=params(),
        cost_estimate=BESIDE,
        name="range_add",
    )(own, far, got)


def base_add_kernel(old_ref, own_ref, out_ref):
    out_ref[...] = old_ref[...] + own_ref[...]


def base_add(old, own):
    vmem = pl.BlockSpec(memory_space=pltpu.VMEM)
    return pl.pallas_call(
        base_add_kernel,
        in_specs=[vmem] * 2,
        out_specs=vmem,
        out_shape=jax.ShapeDtypeStruct(old.shape, F32),
        compiler_params=params(),
        cost_estimate=BESIDE,
        name="base_add",
    )(old, own)


def last_add_kernel(count, old_ref, base_ref, *refs):
    rows = old_ref.shape[0]
    corange_out, range_out = refs[-2:]
    corange_out[...] = old_ref[...] + added([r[0, :rows] for r in refs[:count]])
    range_out[...] = base_ref[...] + added([r[0] for r in refs[count:-2]])


def last_add(old, terms, base, got):
    vmem = pl.BlockSpec(memory_space=pltpu.VMEM)
    return pl.pallas_call(
        functools.partial(last_add_kernel, len(terms)),
        in_specs=[vmem] * (2 + len(terms) + len(got)),
        out_specs=[vmem] * 2,
        out_shape=[jax.ShapeDtypeStruct(a.shape, F32) for a in (old, base)],
        compiler_params=params(),
        cost_estimate=BESIDE,
        name="last_add",
    )(old, base, *terms, *got)


def place_kernel(rows, half, radix, at_ref, old_ref, *refs):
    core, chip = at_ref[0], at_ref[1]
    pieces, out_ref = refs[:-1], refs[-1]
    for i, ref in enumerate(pieces):
        side, digit = i // radix, i % radix
        for g in range(ref.shape[0]):
            row = ((core ^ side) * half + (chip ^ (g * radix + digit))) * rows
            at = pl.ds(pl.multiple_of(row, rows), rows)
            out_ref[at, :] = old_ref[at, :] + ref[g]


def placed(core, chip, old, pieces, parts):
    rows = old.shape[0] // (2 * parts)
    return pl.pallas_call(
        functools.partial(place_kernel, rows, parts, len(pieces) // 2),
        grid_spec=pltpu.PrefetchScalarGridSpec(
            num_scalar_prefetch=1,
            grid=(1,),
            in_specs=[whole(old.shape)] + [whole(p.shape) for p in pieces],
            out_specs=whole(old.shape),
        ),
        out_shape=jax.ShapeDtypeStruct(old.shape, F32),
        compiler_params=params(),
        name="placed",
    )(jnp.stack([core, chip]), old, *pieces)


def stages(chips):
    steps, stride = [], 1
    while stride < chips:
        radix = min(RADIX, chips // stride)
        steps.append((stride, radix))
        stride *= radix
    return steps


def split(value, radix):
    left = value.shape[0] // radix
    value = value.reshape((left, radix) + value.shape[1:])
    return [value[:, k] for k in range(radix)]


def sum_over_chips(terms, series):
    for stride, radix in stages(series // 2):
        if stride > 1:
            terms = [split(t, radix) for t in terms]
        sums = [added(blocks) for blocks in zip(*terms)]
        terms = sums[:1] + [swap(sums[k], "series", 2 * stride * k, series) for k in range(1, radix)]
    return terms


def gather_over_chips(own, series):
    held = [own]
    for stride, radix in reversed(stages(series // 2)):
        if len(held) > 1:
            own = jnp.stack(held, axis=1)
            own = own.reshape((-1,) + own.shape[2:])
        held = [own] + [swap(own, "series", 2 * stride * k, series) for k in range(1, radix)]
    return held


def after(value, *others):
    return lax.optimization_barrier((value,) + others)[0]


def body(series, tm, metric, omega, psi, phi, theta, range_old, corange_old, core_old):
    me = lax.axis_index("series")
    slot = lax.axis_index("tm")
    core, chip = me & 1, me >> 1
    chips = series // 2

    core_send = core_half(1, phi, metric, theta, chips)
    core_got = swap(core_send, "series", 1, series)
    core_keep = core_half(0, after(phi, core_send), metric, theta, chips)
    radix = min(RADIX, chips)
    core_terms = sum_over_chips([split(core_keep, radix), split(core_got, radix)], series)

    near, far, own = range_blocks(slot, after(omega, core_terms[0]), metric, tm)
    range_got = swap(near, "tm", 1, tm)
    corange_send, corange_keep = corange_blocks(core, chip, after(psi, near), metric, chips)
    corange_got = [swap(b, "series", 1, series) for b in corange_send]
    corange_terms = sum_over_chips([corange_keep, corange_got], series)

    core_part = added([after(t, *corange_send) for t in core_terms])
    parts = [core_part] + [swap(core_part, "tm", k, tm) for k in range(1, tm)]

    own, far = range_add(own, after(far, core_part, corange_terms[0]), range_got)
    late = []
    distance = 2
    while distance < tm:
        got = swap(far[::2], "tm", distance, tm)
        late.append(got[:1])
        far = far[1::2] + got[1:]
        distance *= 2
    base = base_add(range_old.T, own)

    parts = [after(p, base) for p in parts]
    while len(parts) > 1:
        parts = [a + b for a, b in zip(parts[::2], parts[1::2])]
    core_all = parts[0]

    corange_new, range_new = last_add(after(corange_old, core_all), corange_terms, base, late)
    pieces = gather_over_chips(core_all, series)
    pieces = pieces[:1] + [after(p, corange_new) for p in pieces[1:]]
    pieces = pieces + [swap(p, "series", 1, series) for p in pieces]
    core_new = placed(core, chip, core_old, pieces, chips)
    return range_new.T, corange_new, core_new


def solution(mesh):
    return jax.shard_map(
        functools.partial(body, mesh.shape["series"], mesh.shape["tm"]),
        mesh=mesh,
        in_specs=(
            P("series", "tm"),
            P("tm", None),
            P(None, "series"),
            P(None, "series"),
            P(None, "tm"),
            P("series", "tm"),
            P(None, ("tm", "series")),
            P(),
        ),
        out_specs=(P("series", "tm"), P(None, ("tm", "series")), P()),
        check_vma=False,
    )
```

```python
import functools
import operator

import jax
import jax.numpy as jnp
from jax import lax
from jax.experimental import pallas as pl
from jax.experimental.pallas import tpu as pltpu
from jax.sharding import PartitionSpec as P

F32 = jnp.float32
RADIX = 4
CHUNKS = 2
DIRECT = True
VMEM_LIMIT = 8 * 1024 * 1024
LAST = pl.CostEstimate(flops=10**6, bytes_accessed=1024 * 1024, transcendentals=0)
LITTLE = pl.CostEstimate(flops=10**6, bytes_accessed=1024, transcendentals=0)
BESIDE = pl.CostEstimate(flops=10**11, bytes_accessed=4 * 1024 * 1024, transcendentals=0)
FIRST_LIMIT = 60 * 1024 * 1024


def added(terms):
    return functools.reduce(operator.add, terms)


def swap(value, axis, bits, size):
    return lax.ppermute(value, axis, [(i, i ^ bits) for i in range(size)])


def params():
    return pltpu.CompilerParams(vmem_limit_bytes=VMEM_LIMIT)


def whole(shape):
    return pl.BlockSpec(shape, lambda i, at: (0,) * len(shape))


def first_kernel(
    parts, phi_any, metric_any, theta_any, omega_any,
    send_ref, keep_ref, near_ref, far_ref, own_ref,
    phi, metric, theta, omega, high, low, sum_ref, range_ref, sems,
):
    me, slot = lax.axis_index("series"), lax.axis_index("tm")
    core, chip = me & 1, me >> 1
    cols = metric.shape[1] // CHUNKS
    copies = [pltpu.make_async_copy(phi_any, phi, sems.at[0])]
    for c in range(CHUNKS):
        at = slice(c * cols, (c + 1) * cols)
        copies.append(
            pltpu.make_async_copy(metric_any.at[:, at], metric.at[:, at], sems.at[1 + c])
        )
    copies.append(pltpu.make_async_copy(theta_any, theta, sems.at[1 + CHUNKS]))
    copies.append(pltpu.make_async_copy(omega_any, omega, sems.at[2 + CHUNKS]))
    for copy in copies:
        copy.start()
    copies[0].wait()
    for c in range(CHUNKS):
        at = slice(c * cols, (c + 1) * cols)
        copies[1 + c].wait()
        left = jnp.dot(phi[...], metric[:, at], preferred_element_type=F32)
        top = left.astype(jnp.bfloat16)
        high[:, at] = top
        low[:, at] = (left - top.astype(F32)).astype(jnp.bfloat16)
    copies[-2].wait()
    copies[-1].wait()
    by_rows = (((1,), (1,)), ((), ()))
    sum_ref[...] = lax.dot_general(high[...], theta[...], by_rows, preferred_element_type=F32)
    sum_ref[...] += lax.dot_general(low[...], theta[...], by_rows, preferred_element_type=F32)
    half = sum_ref.shape[0] // 2
    rows = half // parts
    for ref, side in ((send_ref, 1 - core), (keep_ref, core)):
        for k in range(parts):
            first = pl.multiple_of(side * half + (chip ^ k) * rows, rows)
            ref[k] = sum_ref[pl.ds(first, rows), :]
    range_ref[...] = lax.dot_general(
        omega[...], metric[...], (((0,), (1,)), ((), ())), preferred_element_type=F32
    )
    width = own_ref.shape[0]

    def block(k):
        return range_ref[pl.ds(pl.multiple_of((slot ^ k) * width, width), width), :]

    for j in range(near_ref.shape[0]):
        near_ref[j] = block(2 * j + 1)
    for j in range(far_ref.shape[0]):
        far_ref[j] = block(2 * j + 2)
    own_ref[...] = block(0)


def first_products(phi, metric, theta, omega, parts, slots):
    order, depth = phi.shape
    cols, series, width = theta.shape[0], metric.shape[0], omega.shape[1]
    rows, block = order // 2 // parts, width // slots
    shapes = [(parts, rows, cols)] * 2
    shapes += [(slots // 2, block, series), (slots // 2 - 1, block, series), (block, series)]
    return pl.pallas_call(
        functools.partial(first_kernel, parts),
        in_specs=[pl.BlockSpec(memory_space=pl.ANY)] * 4,
        out_specs=[pl.BlockSpec(memory_space=pltpu.VMEM)] * len(shapes),
        scratch_shapes=[
            pltpu.VMEM(phi.shape, phi.dtype),
            pltpu.VMEM(metric.shape, metric.dtype),
            pltpu.VMEM(theta.shape, theta.dtype),
            pltpu.VMEM(omega.shape, omega.dtype),
            pltpu.VMEM((order, metric.shape[1]), jnp.bfloat16),
            pltpu.VMEM((order, metric.shape[1]), jnp.bfloat16),
            pltpu.VMEM((order, cols), F32),
            pltpu.VMEM((width, series), F32),
            pltpu.SemaphoreType.DMA((CHUNKS + 3,)),
        ],
        out_shape=[jax.ShapeDtypeStruct(s, F32) for s in shapes],
        compiler_params=pltpu.CompilerParams(vmem_limit_bytes=FIRST_LIMIT),
        cost_estimate=pl.CostEstimate(
            flops=2 * depth * metric.shape[1] * (order + width) + 4 * order * cols * metric.shape[1],
            bytes_accessed=4 * 1024 * 1024,
            transcendentals=0,
        ),
        name="first_products",
    )(phi, metric, theta, omega)


def corange_kernel(parts, at_ref, psi_ref, metric_ref, *refs):
    chip, core = at_ref[0], at_ref[1]
    sent, kept, sum_ref = refs[:-1][: len(refs) // 2], refs[:-1][len(refs) // 2 :], refs[-1]
    rows, pair = sum_ref.shape
    cols = pair // 2
    for k in range(parts):
        first = pl.multiple_of((chip ^ k) * pair, pair)
        sum_ref[...] = jnp.dot(
            psi_ref[...], metric_ref[:, pl.ds(first, pair)], preferred_element_type=F32
        )
        for group, side in ((kept, core), (sent, 1 - core)):
            ref, j = group[k % len(group)], k // len(group)
            ref[j, :rows] = sum_ref[:, pl.ds(pl.multiple_of(side * cols, cols), cols)]
            if ref.shape[1] > rows:
                ref[j, rows:] = jnp.zeros((ref.shape[1] - rows, cols), F32)


def corange_blocks(core, chip, psi, metric, parts):
    rows, depth = psi.shape
    cols = metric.shape[1] // (2 * parts)
    radix = min(RADIX, parts)
    if cols % 128:
        term = jnp.dot(psi, metric, preferred_element_type=F32).reshape(rows, parts, 2, cols)
        term = jnp.take(term, chip ^ jnp.arange(parts), axis=1).transpose(2, 1, 0, 3)
        pick = lambda c: split(lax.dynamic_index_in_dim(term, c, 0, keepdims=False), radix)
        return pick(1 - core), pick(core)
    held = -(-rows // 8) * 8
    shape = (parts // radix, held, cols)
    blocks = pl.pallas_call(
        functools.partial(corange_kernel, parts),
        grid_spec=pltpu.PrefetchScalarGridSpec(
            num_scalar_prefetch=1,
            grid=(1,),
            in_specs=[whole(psi.shape), whole(metric.shape)],
            out_specs=[whole(shape)] * (2 * radix),
            scratch_shapes=[pltpu.VMEM((rows, 2 * cols), F32)],
        ),
        out_shape=[jax.ShapeDtypeStruct(shape, F32)] * (2 * radix),
        compiler_params=pltpu.CompilerParams(vmem_limit_bytes=2 * VMEM_LIMIT),
        cost_estimate=BESIDE,
        name="corange_blocks",
    )(jnp.stack([chip, core]), psi, metric)
    return blocks[:radix], blocks[radix:]


def near_add_kernel(old_ref, own_ref, got_ref, out_ref):
    out_ref[...] = old_ref[...] + (own_ref[...] + got_ref[0])


def near_add(old, own, got):
    vmem = pl.BlockSpec(memory_space=pltpu.VMEM)
    return pl.pallas_call(
        near_add_kernel,
        in_specs=[vmem] * 3,
        out_specs=vmem,
        out_shape=jax.ShapeDtypeStruct(old.shape, F32),
        compiler_params=params(),
        cost_estimate=BESIDE,
        name="near_add",
    )(old, own, got)


def far_add_kernel(far_ref, got_ref, out_ref):
    out_ref[...] = far_ref[...] + got_ref[1:]


def far_add(far, got):
    vmem = pl.BlockSpec(memory_space=pltpu.VMEM)
    return pl.pallas_call(
        far_add_kernel,
        in_specs=[vmem] * 2,
        out_specs=vmem,
        out_shape=jax.ShapeDtypeStruct(far.shape, F32),
        compiler_params=params(),
        cost_estimate=LITTLE,
        name="far_add",
    )(far, got)


def corange_add_kernel(old_ref, *refs):
    rows = old_ref.shape[0]
    refs[-1][...] = old_ref[...] + added([r[0, :rows] for r in refs[:-1]])


def corange_add(old, terms):
    vmem = pl.BlockSpec(memory_space=pltpu.VMEM)
    return pl.pallas_call(
        corange_add_kernel,
        in_specs=[vmem] * (1 + len(terms)),
        out_specs=vmem,
        out_shape=jax.ShapeDtypeStruct(old.shape, F32),
        compiler_params=params(),
        cost_estimate=LAST,
        name="corange_add",
    )(old, *terms)


def place_kernel(rows, half, radix, at_ref, old_ref, *refs):
    core, chip = at_ref[0], at_ref[1]
    pieces, out_ref = refs[:-1], refs[-1]
    for i, ref in enumerate(pieces):
        side, digit = i // radix, i % radix
        for g in range(ref.shape[0]):
            row = ((core ^ side) * half + (chip ^ (g * radix + digit))) * rows
            at = pl.ds(pl.multiple_of(row, rows), rows)
            out_ref[at, :] = old_ref[at, :] + ref[g]


def placed(core, chip, old, pieces, parts):
    rows = old.shape[0] // (2 * parts)
    return pl.pallas_call(
        functools.partial(place_kernel, rows, parts, len(pieces) // 2),
        grid_spec=pltpu.PrefetchScalarGridSpec(
            num_scalar_prefetch=1,
            grid=(1,),
            in_specs=[whole(old.shape)] + [whole(p.shape) for p in pieces],
            out_specs=whole(old.shape),
        ),
        out_shape=jax.ShapeDtypeStruct(old.shape, F32),
        compiler_params=params(),
        name="placed",
    )(jnp.stack([core, chip]), old, *pieces)


def stages(chips):
    steps, stride = [], 1
    while stride < chips:
        radix = min(RADIX, chips // stride)
        steps.append((stride, radix))
        stride *= radix
    return steps


def split(value, radix):
    left = value.shape[0] // radix
    value = value.reshape((left, radix) + value.shape[1:])
    return [value[:, k] for k in range(radix)]


def sum_over_chips(terms, series):
    for stride, radix in stages(series // 2):
        if stride > 1:
            terms = [split(t, radix) for t in terms]
        sums = [added(blocks) for blocks in zip(*terms)]
        terms = sums[:1] + [swap(sums[k], "series", 2 * stride * k, series) for k in range(1, radix)]
    return terms


def gather_over_chips(own, series):
    held = [own]
    for stride, radix in reversed(stages(series // 2)):
        if len(held) > 1:
            own = jnp.stack(held, axis=1)
            own = own.reshape((-1,) + own.shape[2:])
        held = [own] + [swap(own, "series", 2 * stride * k, series) for k in range(1, radix)]
    return held


def after(value, *others):
    return lax.optimization_barrier((value,) + others)[0]


def body(series, tm, metric, omega, psi, phi, theta, range_old, corange_old, core_old):
    me = lax.axis_index("series")
    slot = lax.axis_index("tm")
    core, chip = me & 1, me >> 1
    chips = series // 2

    core_send, core_keep, near, far, own = first_products(phi, metric, theta, omega, chips, tm)
    core_got = swap(core_send, "series", 1, series)
    range_got = swap(near, "tm", 1, tm)
    radix = min(RADIX, chips)
    core_terms = sum_over_chips([split(core_keep, radix), split(core_got, radix)], series)

    corange_send, corange_keep = corange_blocks(core, chip, after(psi, core_terms[0]), metric, chips)
    corange_got = [swap(b, "series", 1, series) for b in corange_send]
    corange_terms = sum_over_chips([corange_keep, corange_got], series)

    core_part = added([after(t, *corange_send) for t in core_terms])

    got = swap(core_part, "tm", 1, tm)
    base = near_add(range_old.T, after(own, core_part, corange_terms[0]), range_got)
    core_all = core_part + after(got, base)
    distance = 2
    while distance < tm:
        core_all = core_all + swap(core_all, "tm", distance, tm)
        distance *= 2

    far = far_add(after(far, core_all), range_got)
    late = []
    distance = 2
    while distance < tm:
        got = swap(far[::2], "tm", distance, tm)
        late.append(got[:1])
        far = far[1::2] + got[1:]
        distance *= 2

    corange_new = corange_add(after(corange_old, core_all), corange_terms)
    pieces = gather_over_chips(core_all, series)
    pieces = pieces[:1] + [after(p, corange_new) for p in pieces[1:]]
    pieces = pieces + [swap(p, "series", 1, series) for p in pieces]
    core_new = placed(core, chip, core_old, pieces, chips)
    range_new = (base + added([g[0] for g in late])).T
    return range_new, corange_new, core_new


def solution(mesh):
    return jax.shard_map(
        functools.partial(body, mesh.shape["series"], mesh.shape["tm"]),
        mesh=mesh,
        in_specs=(
            P("series", "tm"),
            P("tm", None),
            P(None, "series"),
            P(None, "series"),
            P(None, "tm"),
            P("series", "tm"),
            P(None, ("tm", "series")),
            P(),
        ),
        out_specs=(P("series", "tm"), P(None, ("tm", "series")), P()),
        check_vma=False,
    )
```
